32 devices in a mesh: parts: 1, node: 2 (over core), local: 16 (over z, y, x).
Axes of the slice: x: 2, y: 2, z: 4, core: 2. Of those that a mesh axis runs over, the one named last changes fastest.
Arguments:
- tokens: bfloat16 [2048, 3584], P(('parts', 'node', 'local')), may hold values from -6 to 6
- routes: int32 [2048, 8], P(('parts', 'node', 'local')), may hold values from 0 to 15, as said below
- gate_weights: float32 [2048, 8], P(('parts', 'node', 'local')), may hold values from 0.1 to 1
- gate_proj: bfloat16 [32, 3584, 512], P(('node', 'local')), may hold values from -0.09375 to 0.09375
- up_proj: bfloat16 [32, 3584, 512], P(('node', 'local')), may hold values from -0.09375 to 0.09375
- down_proj: bfloat16 [32, 1024, 1792], P(('node', 'local')), may hold values from -0.1875 to 0.1875
Outputs:
- combined: bfloat16 [2048, 3584], P(('parts', 'node', 'local'))
The draws below stay inside these ranges and needn't reach their ends.
Inputs may be any that keep to these rules, and one draw needn't show every extreme that they name: `routes`: group g is experts 4g to 4g + 3. Each row names 8 different experts, 2 in each of exactly 4 groups. Among the 64 rows of one device each group is chosen by exactly 64 rows, and no expert is named more than 40 times; in every device's rows some expert is named exactly 40 times.
All inputs are finite; a program needn't handle non-finite values.
Results may differ from the reference program's by a relative error of at most 0.0059.
Values may be sent and summed in bfloat16 or wider, within the bound.
A program may use at most 128 MiB of HBM per device.

```python
import math
import jax
import jax.numpy as jnp
from jax import lax

D = 3584
FF = 1024
TOPK = 8
LIMIT = 4
TOK_DEV = 64
EXPERTS = 16
GROUPS = 4
CAP = 40
TOKENS = 2048
N_NODE = 2
N_LOCAL = 16


def permute_each(key, count, length):
    keys = jax.random.split(key, count)
    return jax.vmap(lambda single: jax.random.permutation(single, length))(keys).astype(jnp.int32)


def draw_routes(key, part):
    key = jax.random.fold_in(key, 11)
    blocks = TOKENS // TOK_DEV
    per_group = TOK_DEV // GROUPS
    visits = TOK_DEV * LIMIT // GROUPS
    pick = TOPK // LIMIT
    rest = pick * visits - CAP
    second = rest // 3 + min(rest % 3, 1)
    third = rest // 3 + min(max(rest % 3 - 1, 0), 1)
    bounds = jnp.array([CAP, CAP + second, CAP + second + third], jnp.int32)
    key_a, key_b, key_c, key_d = jax.random.split(key, 4)
    group_perm = permute_each(key_a, blocks, GROUPS)
    row_perm = permute_each(key_b, blocks, TOK_DEV)
    visit_perm = permute_each(key_c, blocks * GROUPS, visits).reshape(blocks, GROUPS, visits)
    expert_perm = permute_each(key_d, blocks * GROUPS, 4).reshape(blocks, GROUPS, 4)
    row_base = row_perm // GROUPS
    row_cycle = row_perm % GROUPS
    choice_idx = jnp.arange(LIMIT, dtype=jnp.int32)
    position = (row_cycle[:, :, None] + choice_idx[None, None, :]) % GROUPS
    group = jnp.take_along_axis(group_perm, position.reshape(blocks, TOK_DEV * LIMIT), axis=1).reshape(blocks, TOK_DEV, LIMIT)
    visit = choice_idx[None, None, :] * per_group + row_base[:, :, None]
    block_idx = jnp.arange(blocks, dtype=jnp.int32)[:, None, None]
    shuffled = visit_perm[block_idx, group, visit]
    spots = shuffled[..., None] + jnp.arange(pick, dtype=jnp.int32) * visits
    rank = jnp.sum((spots[..., None] >= bounds).astype(jnp.int32), axis=-1)
    chosen = 4 * group[..., None] + expert_perm[block_idx[..., None], group[..., None], rank]
    return chosen.reshape(TOKENS, TOPK).astype(jnp.int32)


def steps_of(rng, extent, shards, low, largest):
    def one(dim, shards_of):
        heights = jax.random.uniform(jax.random.fold_in(jax.random.fold_in(rng, 6), dim), (shards_of,), jnp.float32, low / len(shards), largest / len(shards))
        return jnp.repeat(jnp.exp(heights), extent[dim] // shards_of).reshape((-1,) + (1,) * (len(extent) - dim - 1))

    loudness = one(*shards[0])
    for cut in shards[1:]:
        loudness = loudness * one(*cut)
    return loudness


def gaussian(key, extent, deviation, reach, pieces=(), kind=jnp.bfloat16):
    gain = steps_of(key, extent, pieces, -0.22, 0.18) if pieces else 1.0
    values = jax.random.normal(key, extent, jnp.float32) * deviation * gain
    return jnp.minimum(jnp.maximum(values, -reach), reach).astype(kind)


def setup_inputs(seed: int = 0, part: int = 0) -> dict:
    key_list = jax.random.split(jax.random.key(seed), 7)
    part_splits = jax.random.split(jax.random.fold_in(key_list[6], part), 7)
    tokens = gaussian(part_splits[0], (TOKENS, D), 1.0, 6.0, ((0, 32),))
    routes = draw_routes(jax.random.fold_in(jax.random.fold_in(key_list[6], part), 71), part)
    gate_weights = jnp.clip(jnp.exp(math.log(1.0) - 2.3025851 * jax.random.uniform(part_splits[2], (TOKENS, TOPK), jnp.float32) ** steps_of(part_splits[2], (TOKENS, TOPK), ((0, 32),), -0.2, 0.2)), 0.1, 1.0)
    gate_proj = gaussian(key_list[3], (2 * EXPERTS, D, FF // 2), D ** -0.5, 0.09375, ((0, 32),))
    up_proj = gaussian(key_list[4], (2 * EXPERTS, D, FF // 2), D ** -0.5, 0.09375, ((0, 32),))
    down_proj = gaussian(key_list[5], (2 * EXPERTS, FF, D // 2), FF ** -0.5, 0.1875, ((0, 32),))
    return {"tokens": tokens, "routes": routes, "gate_weights": gate_weights, "gate_proj": gate_proj, "up_proj": up_proj, "down_proj": down_proj}


def reference(tokens, routes, gate_weights, gate_proj, up_proj, down_proj):
    pair_count = TOKENS * TOPK
    route_list = routes.reshape(-1).astype(jnp.int32)
    indicator = (route_list[:, None] == jnp.arange(EXPERTS, dtype=jnp.int32)[None, :]).astype(jnp.int32)
    earlier = jnp.cumsum(indicator, axis=0) - indicator
    slot_rank = jnp.sum(earlier * indicator, axis=1).astype(jnp.int32)
    depth = CAP * N_NODE * N_LOCAL
    table = jnp.full((EXPERTS, depth), pair_count, jnp.int32)
    table = table.at[route_list, slot_rank].set(jnp.arange(pair_count, dtype=jnp.int32))
    padded_tokens = jnp.concatenate([tokens, jnp.zeros((1, D), tokens.dtype)], axis=0)

    def one_expert(index):
        pair_ids = table[index]
        token_ids = (pair_ids // TOPK).astype(jnp.int32)
        row_block = padded_tokens[token_ids]
        gate_matrix = jnp.concatenate([gate_proj[2 * index], gate_proj[2 * index + 1]], axis=1)
        up_matrix = jnp.concatenate([up_proj[2 * index], up_proj[2 * index + 1]], axis=1)
        down_matrix = jnp.concatenate([down_proj[2 * index], down_proj[2 * index + 1]], axis=1)
        gate_act = jnp.dot(row_block, gate_matrix, preferred_element_type=jnp.float32)
        up_act = jnp.dot(row_block, up_matrix, preferred_element_type=jnp.float32)
        hidden = (jax.nn.silu(gate_act) * up_act).astype(jnp.bfloat16)
        return jnp.dot(hidden, down_matrix, preferred_element_type=jnp.float32).astype(jnp.bfloat16)

    outputs = lax.map(one_expert, jnp.arange(EXPERTS, dtype=jnp.int32))
    per_pair = outputs[route_list, slot_rank].reshape(TOKENS, TOPK, D)
    combined = jnp.sum(gate_weights[:, :, None] * per_pair.astype(jnp.float32), axis=1)
    return combined.astype(jnp.bfloat16)
```

```python
import jax
import jax.numpy as jnp
from jax import lax
from jax.sharding import Mesh, PartitionSpec as P


def per_device(tokens, routes, gate_weights, gate_proj, up_proj, down_proj):
    node_count = lax.axis_size("node")
    pair_count = lax.axis_size("pair")
    experts = node_count * pair_count
    spread = ("node", "pair", "half")
    expert_ids = jnp.arange(experts, dtype=jnp.int32)
    chosen = routes[:, :, None] == expert_ids[None, None, :]
    weight_table = jnp.sum(jnp.where(chosen, gate_weights[:, :, None], 0.0), axis=1)
    all_tokens = lax.all_gather(tokens, spread, axis=0, tiled=True)
    all_weights = lax.all_gather(weight_table, spread, axis=0, tiled=True)
    expert = lax.axis_index("node") * pair_count + lax.axis_index("pair")
    weight = jnp.sum(jnp.where(expert_ids[None, :] == expert, all_weights, 0.0), axis=1)
    gate_act = jnp.dot(all_tokens, gate_proj[0], preferred_element_type=jnp.float32)
    up_act = jnp.dot(all_tokens, up_proj[0], preferred_element_type=jnp.float32)
    own_half = (jax.nn.silu(gate_act) * up_act).astype(jnp.bfloat16)
    other_half = lax.ppermute(own_half, "half", [(0, 1), (1, 0)])
    half = lax.axis_index("half")
    depth = own_half.shape[1]
    own_down = lax.dynamic_slice_in_dim(down_proj[0], half * depth, depth, 0)
    other_down = lax.dynamic_slice_in_dim(down_proj[0], (1 - half) * depth, depth, 0)
    out = jnp.dot(own_half, own_down, preferred_element_type=jnp.float32) + jnp.dot(
        other_half, other_down, preferred_element_type=jnp.float32
    )
    part = (weight[:, None] * out.astype(jnp.bfloat16).astype(jnp.float32)).astype(jnp.bfloat16)
    summed = lax.psum_scatter(part, ("node", "pair"), scatter_dimension=0, tiled=True)
    return lax.all_to_all(summed, "half", split_axis=0, concat_axis=1, tiled=True)


def solution(mesh):
    sizes = dict(mesh.shape)
    devices = mesh.devices.reshape(sizes["parts"], sizes["node"], sizes["local"] // 2, 2)
    split = Mesh(devices, ("parts", "node", "pair", "half"))
    rows = P(("parts", "node", "pair", "half"), None)
    blocks = P(("node", "pair", "half"), None, None)
    return jax.shard_map(
        per_device,
        mesh=split,
        in_specs=(rows, rows, rows, blocks, blocks, blocks),
        out_specs=rows,
        check_vma=False,
    )
```

```python
import functools

import jax
import jax.numpy as jnp
from jax import lax
from jax.experimental import pallas as pl
from jax.experimental.pallas import tpu as pltpu
from jax.sharding import Mesh, PartitionSpec as P

MESH = pl.DeviceIdType.MESH


def gather_kernel(
    depth, width, tok, gate, up, own_out, other_out, weight_out,
    buf, hid, gate_v, up_v,
    z_send, z_recv, x_send, x_recv, y_send, y_recv, s_send, s_recv,
    d_send, d_recv, load_sem, h_send, h_recv, o_sem, w_sem,
):
    p = lax.axis_index("parts")
    n = lax.axis_index("node")
    z = lax.axis_index("z")
    y = lax.axis_index("y")
    x = lax.axis_index("half")
    rows = tok.shape[0]
    sibling = (p, 1 - n, z, y, x)
    x_side = (p, n, z, y, 1 - x)
    y_side = (p, n, z, 1 - y, x)
    z_peers = [(p, n, lax.rem(z + step, depth), y, x) for step in range(1, depth)]

    barrier = pltpu.get_barrier_semaphore()
    for peer in [sibling, x_side, y_side] + z_peers:
        pl.semaphore_signal(barrier, inc=1, device_id=peer, device_id_type=MESH)
    pl.semaphore_wait(barrier, depth + 2)

    def remote(src, dst, send, recv, peer):
        return pltpu.make_async_remote_copy(
            src_ref=src, dst_ref=dst, send_sem=send, recv_sem=recv,
            device_id=peer, device_id_type=MESH,
        )

    def place(core, k, step):
        return buf.at[
            core, lax.rem(y + k // 2, 2), lax.rem(x + k % 2, 2), lax.rem(z - step + depth, depth)
        ]

    via_x = [step for step in range(depth) if step < depth // 4]

    def send_z(step):
        return remote(tok, place(n, 0, 0), z_send.at[step], z_recv.at[step], z_peers[step - 1])

    def recv_z(step):
        ref = place(n, 0, step)
        return remote(ref, ref, z_send.at[step], z_recv.at[step], sibling)

    def send_x(step):
        src = tok if step == 0 else place(n, 0, step)
        return remote(src, place(n, 0, step), x_send.at[step], x_recv.at[step], x_side)

    def send_y(step):
        src = tok if step == 0 else place(n, 0, step)
        return remote(src, place(n, 0, step), y_send.at[step], y_recv.at[step], y_side)

    def send_s(k, step):
        src = tok if (k == 0 and step == 0) else place(n, k, step)
        return remote(src, place(n, k, step), s_send.at[k, step], s_recv.at[k, step], sibling)

    def send_d(step):
        if step in via_x:
            ref, peer = place(n, 2, step), x_side
        else:
            ref, peer = place(n, 1, step), y_side
        return remote(ref, ref, d_send.at[step], d_recv.at[step], peer)

    def arrive(core, k, step, send, recv):
        ref = place(core, k, step)
        remote(ref, ref, send, recv, sibling).wait_recv()

    for step in range(1, depth):
        send_z(step).start()
    send_x(0).start()
    send_y(0).start()
    send_s(0, 0).start()
    own_copy = pltpu.make_async_copy(tok, place(n, 0, 0), load_sem.at[0])
    own_copy.start()
    gate_copy = pltpu.make_async_copy(gate, gate_v, load_sem.at[1])
    gate_copy.start()
    up_copy = pltpu.make_async_copy(up, up_v, load_sem.at[2])
    up_copy.start()

    def hid_copy(slot, core, yy, xx):
        return remote(
            hid.at[slot], other_out.at[core, :, yy, xx], h_send.at[slot], h_recv.at[slot], x_side
        )

    def out_copy(slot, core, yy, xx):
        return pltpu.make_async_copy(hid.at[slot], own_out.at[core, :, yy, xx], o_sem.at[slot])

    def weight_copy(slot, core, yy, xx):
        return pltpu.make_async_copy(
            buf.at[core, yy, xx, :, :, pl.ds(width, 128)],
            weight_out.at[core, :, yy, xx],
            w_sem.at[slot],
        )

    def group_of(slot):
        k = slot // 2
        core = lax.rem(n + slot % 2, 2)
        return core, lax.rem(y + k // 2, 2), lax.rem(x + k % 2, 2)

    def work(first, last):
        @pl.loop(first, last)
        def _(slot):
            core, yy, xx = group_of(slot)

            @pl.when(slot % 2 == 1)
            def _():
                for step in range(depth):
                    arrive(1 - n, slot // 2, step, s_send.at[slot // 2, step], s_recv.at[slot // 2, step])

            block = buf[core, yy, xx, :, :, pl.ds(0, width)].reshape(depth * rows, width)
            gate_act = jnp.dot(block, gate_v[...], preferred_element_type=jnp.float32)
            up_act = jnp.dot(block, up_v[...], preferred_element_type=jnp.float32)
            hidden = gate_act / (1.0 + jnp.exp(-gate_act)) * up_act
            hid[slot] = hidden.astype(jnp.bfloat16).reshape(depth, rows, hidden.shape[1])
            hid_copy(slot, core, yy, xx).start()
            out_copy(slot, core, yy, xx).start()
            weight_copy(slot, core, yy, xx).start()

    for step in range(1, depth + 2):
        if step < depth:
            recv_z(step).wait_recv()
            send_x(step).start()
            send_y(step).start()
            send_s(0, step).start()
        if 1 <= step <= depth:
            late = step - 1
            arrive(n, 1, late, x_send.at[late], x_recv.at[late])
            if late not in via_x:
                send_d(late).start()
            send_s(1, late).start()
            arrive(n, 2, late, y_send.at[late], y_recv.at[late])
            if late in via_x:
                send_d(late).start()
            send_s(2, late).start()
        if step >= 2:
            late = step - 2
            arrive(n, 3, late, d_send.at[late], d_recv.at[late])
            send_s(3, late).start()
        if step == depth - 1:
            own_copy.wait()
            gate_copy.wait()
            up_copy.wait()
            work(0, 2)
        if step == depth:
            work(2, 6)
    work(6, 8)

    for step in range(1, depth):
        send_z(step).wait_send()
    for step in range(depth):
        send_x(step).wait_send()
        send_y(step).wait_send()
        send_d(step).wait_send()
        for k in range(4):
            send_s(k, step).wait_send()

    @pl.loop(0, 8)
    def _(slot):
        core, yy, xx = group_of(slot)
        hid_copy(slot, core, yy, xx).wait_send()
        hid_copy(slot, core, yy, lax.rem(xx + 1, 2)).wait_recv()
        out_copy(slot, core, yy, xx).wait()
        weight_copy(slot, core, yy, xx).wait()


def gather_hidden(packed, gate, up, depth):
    rows, wide = packed.shape
    width, units = gate.shape
    grid = (2, depth, 2, 2, rows)
    dma = pltpu.SemaphoreType.DMA
    any_spec = pl.BlockSpec(memory_space=pl.ANY)
    total = 8 * depth * rows
    return pl.pallas_call(
        functools.partial(gather_kernel, depth, width),
        out_shape=(
            jax.ShapeDtypeStruct(grid + (units,), jnp.bfloat16),
            jax.ShapeDtypeStruct(grid + (units,), jnp.bfloat16),
            jax.ShapeDtypeStruct(grid + (128,), jnp.bfloat16),
        ),
        in_specs=[any_spec] * 3,
        out_specs=(any_spec,) * 3,
        scratch_shapes=[
            pltpu.VMEM((2, 2, 2, depth, rows, wide), jnp.bfloat16),
            pltpu.VMEM((8, depth, rows, units), jnp.bfloat16),
            pltpu.VMEM((width, units), jnp.bfloat16),
            pltpu.VMEM((width, units), jnp.bfloat16),
            dma((depth,)), dma((depth,)), dma((depth,)), dma((depth,)), dma((depth,)), dma((depth,)),
            dma((4, depth)), dma((4, depth)), dma((depth,)), dma((depth,)),
            dma((3,)), dma((8,)), dma((8,)), dma((8,)), dma((8,)),
        ],
        cost_estimate=pl.CostEstimate(
            flops=4 * total * width * units, bytes_accessed=2 * total * wide, transcendentals=total * units
        ),
        compiler_params=pltpu.CompilerParams(
            collective_id=0, has_side_effects=True, vmem_limit_bytes=56 * 1024 * 1024
        ),
    )(packed, gate, up)


def per_device(tokens, routes, gate_weights, gate_proj, up_proj, down_proj):
    depth = lax.axis_size("z")
    pair_count = 2 * depth
    experts = 2 * pair_count
    rows = tokens.shape[0]
    expert_ids = jnp.arange(experts, dtype=jnp.int32)
    chosen = routes[:, :, None] == expert_ids[None, None, :]
    table = jnp.sum(jnp.where(chosen, gate_weights[:, :, None], 0.0), axis=1)
    high = lax.reduce_precision(table, 8, 7)
    middle = lax.reduce_precision(table - high, 8, 7)
    low = table - high - middle
    spare = jnp.zeros((rows, 128 - 3 * experts), jnp.float32)
    columns = jnp.concatenate([high, middle, low, spare], axis=1).astype(jnp.bfloat16)
    packed = jnp.concatenate([tokens, columns], axis=1)
    own_half, other_half, weights = gather_hidden(packed, gate_proj[0], up_proj[0], depth)
    units = own_half.shape[-1]
    own_half = own_half.reshape(-1, units)
    other_half = other_half.reshape(-1, units)
    weights = weights.reshape(-1, 128).astype(jnp.float32)
    expert = (lax.axis_index("node") * depth + lax.axis_index("z")) * 2 + lax.axis_index("y")
    lane = jnp.arange(128, dtype=jnp.int32)
    mine = (lane % experts == expert) & (lane < 3 * experts)
    weight = jnp.sum(jnp.where(mine[None, :], weights, 0.0), axis=1)
    half = lax.axis_index("half")
    own_down = lax.dynamic_slice_in_dim(down_proj[0], half * units, units, 0)
    other_down = lax.dynamic_slice_in_dim(down_proj[0], (1 - half) * units, units, 0)
    out = jnp.dot(own_half, own_down, preferred_element_type=jnp.float32) + jnp.dot(
        other_half, other_down, preferred_element_type=jnp.float32
    )
    part = (weight[:, None] * out.astype(jnp.bfloat16).astype(jnp.float32)).astype(jnp.bfloat16)
    summed = lax.psum_scatter(part, ("node", "z", "y"), scatter_dimension=0, tiled=True)
    return lax.all_to_all(summed, "half", split_axis=0, concat_axis=1, tiled=True)


def solution(mesh):
    sizes = dict(mesh.shape)
    devices = mesh.devices.reshape(sizes["parts"], sizes["node"], sizes["local"] // 4, 2, 2)
    split = Mesh(devices, ("parts", "node", "z", "y", "half"))
    rows = P(("parts", "node", "z", "y", "half"), None)
    blocks = P(("node", "z", "y", "half"), None, None)
    return jax.shard_map(
        per_device,
        mesh=split,
        in_specs=(rows, rows, rows, blocks, blocks, blocks),
        out_specs=rows,
        check_vma=False,
    )
```

```python
import functools

import jax
import jax.numpy as jnp
from jax import lax
from jax.experimental import pallas as pl
from jax.experimental.pallas import tpu as pltpu
from jax.sharding import Mesh, PartitionSpec as P

MESH = pl.DeviceIdType.MESH


def gather_kernel(
    depth, width, tok, gate, up, own_out, other_out, weight_out,
    buf, hid, gate_v, up_v,
    z_send, z_recv, x_send, x_recv, y_send, y_recv, s_send, s_recv,
    d_send, d_recv, load_sem, h_send, h_recv, o_sem, w_sem,
):
    p = lax.axis_index("parts")
    n = lax.axis_index("node")
    z = lax.axis_index("z")
    y = lax.axis_index("y")
    x = lax.axis_index("half")
    rows = tok.shape[0]
    sibling = (p, 1 - n, z, y, x)
    x_side = (p, n, z, y, 1 - x)
    y_side = (p, n, z, 1 - y, x)
    z_peers = [(p, n, lax.rem(z + step, depth), y, x) for step in range(1, depth)]

    barrier = pltpu.get_barrier_semaphore()
    for peer in [sibling, x_side, y_side] + z_peers:
        pl.semaphore_signal(barrier, inc=1, device_id=peer, device_id_type=MESH)
    pl.semaphore_wait(barrier, depth + 2)

    def remote(src, dst, send, recv, peer):
        return pltpu.make_async_remote_copy(
            src_ref=src, dst_ref=dst, send_sem=send, recv_sem=recv,
            device_id=peer, device_id_type=MESH,
        )

    def place(core, k, step):
        return buf.at[
            core, lax.rem(y + k // 2, 2), lax.rem(x + k % 2, 2), lax.rem(z - step + depth, depth)
        ]

    via_x = [step for step in range(depth) if step < depth // 4]

    def send_z(step):
        return remote(tok, place(n, 0, 0), z_send.at[step], z_recv.at[step], z_peers[step - 1])

    def recv_z(step):
        ref = place(n, 0, step)
        return remote(ref, ref, z_send.at[step], z_recv.at[step], sibling)

    def send_x(step):
        src = tok if step == 0 else place(n, 0, step)
        return remote(src, place(n, 0, step), x_send.at[step], x_recv.at[step], x_side)

    def send_y(step):
        src = tok if step == 0 else place(n, 0, step)
        return remote(src, place(n, 0, step), y_send.at[step], y_recv.at[step], y_side)

    def send_s(k, step):
        src = tok if (k == 0 and step == 0) else place(n, k, step)
        return remote(src, place(n, k, step), s_send.at[k, step], s_recv.at[k, step], sibling)

    def send_d(step):
        if step in via_x:
            ref, peer = place(n, 2, step), x_side
        else:
            ref, peer = place(n, 1, step), y_side
        return remote(ref, ref, d_send.at[step], d_recv.at[step], peer)

    def arrive(core, k, step, send, recv):
        ref = place(core, k, step)
        remote(ref, ref, send, recv, sibling).wait_recv()

    for step in range(1, depth):
        send_z(step).start()
    send_x(0).start()
    send_y(0).start()
    send_s(0, 0).start()
    own_copy = pltpu.make_async_copy(tok, place(n, 0, 0), load_sem.at[0])
    own_copy.start()
    gate_copy = pltpu.make_async_copy(gate, gate_v, load_sem.at[1])
    gate_copy.start()
    up_copy = pltpu.make_async_copy(up, up_v, load_sem.at[2])
    up_copy.start()

    def hid_copy(slot, core, yy, xx):
        return remote(
            hid.at[slot], other_out.at[core, :, yy, xx], h_send.at[slot], h_recv.at[slot], x_side
        )

    def out_copy(slot, core, yy, xx):
        return pltpu.make_async_copy(hid.at[slot], own_out.at[core, :, yy, xx], o_sem.at[slot])

    def weight_copy(slot, core, yy, xx):
        return pltpu.make_async_copy(
            buf.at[core, yy, xx, :, :, pl.ds(width, 128)],
            weight_out.at[core, :, yy, xx],
            w_sem.at[slot],
        )

    def group_of(slot):
        k = slot // 2
        core = lax.rem(n + slot % 2, 2)
        return core, lax.rem(y + k // 2, 2), lax.rem(x + k % 2, 2)

    def work(first, last):
        @pl.loop(first, last)
        def _(slot):
            core, yy, xx = group_of(slot)

            @pl.when(slot % 2 == 1)
            def _():
                for step in range(depth):
                    arrive(1 - n, slot // 2, step, s_send.at[slot // 2, step], s_recv.at[slot // 2, step])

            block = buf[core, yy, xx, :, :, pl.ds(0, width)].reshape(depth * rows, width)
            gate_act = jnp.dot(block, gate_v[...], preferred_element_type=jnp.float32)
            up_act = jnp.dot(block, up_v[...], preferred_element_type=jnp.float32)
            hidden = gate_act / (1.0 + jnp.exp(-gate_act)) * up_act
            hid[slot] = hidden.astype(jnp.bfloat16).reshape(depth, rows, hidden.shape[1])
            hid_copy(slot, core, yy, xx).start()
            out_copy(slot, core, yy, xx).start()
            weight_copy(slot, core, yy, xx).start()

    for step in range(1, depth + 2):
        if step < depth:
            recv_z(step).wait_recv()
            send_x(step).start()
            send_y(step).start()
            send_s(0, step).start()
        if 1 <= step <= depth:
            late = step - 1
            arrive(n, 1, late, x_send.at[late], x_recv.at[late])
            if late not in via_x:
                send_d(late).start()
            send_s(1, late).start()
            arrive(n, 2, late, y_send.at[late], y_recv.at[late])
            if late in via_x:
                send_d(late).start()
            send_s(2, late).start()
        if step >= 2:
            late = step - 2
            arrive(n, 3, late, d_send.at[late], d_recv.at[late])
            send_s(3, late).start()
        if step == depth - 1:
            own_copy.wait()
            gate_copy.wait()
            up_copy.wait()
            work(0, 2)
        if step == depth:
            work(2, 6)
    work(6, 8)

    for step in range(1, depth):
        send_z(step).wait_send()
    for step in range(depth):
        send_x(step).wait_send()
        send_y(step).wait_send()
        send_d(step).wait_send()
        for k in range(4):
            send_s(k, step).wait_send()

    @pl.loop(0, 8)
    def _(slot):
        core, yy, xx = group_of(slot)
        hid_copy(slot, core, yy, xx).wait_send()
        hid_copy(slot, core, yy, lax.rem(xx + 1, 2)).wait_recv()
        out_copy(slot, core, yy, xx).wait()
        weight_copy(slot, core, yy, xx).wait()


def gather_hidden(packed, gate, up, depth):
    rows, wide = packed.shape
    width, units = gate.shape
    grid = (2, depth, 2, 2, rows)
    dma = pltpu.SemaphoreType.DMA
    any_spec = pl.BlockSpec(memory_space=pl.ANY)
    total = 8 * depth * rows
    return pl.pallas_call(
        functools.partial(gather_kernel, depth, width),
        out_shape=(
            jax.ShapeDtypeStruct(grid + (units,), jnp.bfloat16),
            jax.ShapeDtypeStruct(grid + (units,), jnp.bfloat16),
            jax.ShapeDtypeStruct(grid + (128,), jnp.bfloat16),
        ),
        in_specs=[any_spec] * 3,
        out_specs=(any_spec,) * 3,
        scratch_shapes=[
            pltpu.VMEM((2, 2, 2, depth, rows, wide), jnp.bfloat16),
            pltpu.VMEM((8, depth, rows, units), jnp.bfloat16),
            pltpu.VMEM((width, units), jnp.bfloat16),
            pltpu.VMEM((width, units), jnp.bfloat16),
            dma((depth,)), dma((depth,)), dma((depth,)), dma((depth,)), dma((depth,)), dma((depth,)),
            dma((4, depth)), dma((4, depth)), dma((depth,)), dma((depth,)),
            dma((3,)), dma((8,)), dma((8,)), dma((8,)), dma((8,)),
        ],
        cost_estimate=pl.CostEstimate(
            flops=4 * total * width * units, bytes_accessed=2 * total * wide, transcendentals=total * units
        ),
        compiler_params=pltpu.CompilerParams(
            collective_id=0, has_side_effects=True, vmem_limit_bytes=56 * 1024 * 1024
        ),
    )(packed, gate, up)


def combine_kernel(
    depth, experts, own, other, weights, down, out,
    a_out, a_in, acc, keep, y_out, y_in, z_out, z_in, f_out, f_in,
    a_send, a_recv, y_send, y_recv, z_send, z_recv, f_send, f_recv,
):
    p = lax.axis_index("parts")
    n = lax.axis_index("node")
    z = lax.axis_index("z")
    y = lax.axis_index("y")
    x = lax.axis_index("half")
    rows, units = own.shape[4:]
    width = down.shape[1]
    sibling = (p, 1 - n, z, y, x)
    x_side = (p, n, z, y, 1 - x)
    y_side = (p, n, z, 1 - y, x)

    barrier = pltpu.get_barrier_semaphore()
    for peer in [sibling, x_side, y_side] + [
        (p, n, lax.rem(z + step, depth), y, x) for step in range(1, depth)
    ]:
        pl.semaphore_signal(barrier, inc=1, device_id=peer, device_id_type=MESH)
    pl.semaphore_wait(barrier, depth + 2)

    def remote(src, dst, send, recv, peer):
        return pltpu.make_async_remote_copy(
            src_ref=src, dst_ref=dst, send_sem=send, recv_sem=recv,
            device_id=peer, device_id_type=MESH,
        )

    def send_a(t):
        return remote(a_out.at[t], a_in.at[t], a_send.at[t], a_recv.at[t], sibling)

    def send_y(t):
        return remote(y_out.at[t], y_in.at[t], y_send.at[t], y_recv.at[t], y_side)

    def send_z(t):
        peer = (p, n, lax.rem(z + 1 + t, depth), y, x)
        return remote(z_out.at[t], z_in.at[t], z_send.at[t], z_recv.at[t], peer)

    expert = (n * depth + z) * 2 + y
    lane = lax.broadcasted_iota(jnp.int32, (4 * rows, 128), 1)
    mine = (lane == expert) | (lane == expert + experts) | (lane == expert + 2 * experts)

    def weighted(core, zz):
        own_down = down[pl.ds(pl.multiple_of(x * units, units), units), :]
        other_down = down[pl.ds(pl.multiple_of((1 - x) * units, units), units), :]
        value = jnp.dot(
            own[core, zz].reshape(4 * rows, units), own_down, preferred_element_type=jnp.float32
        ) + jnp.dot(
            other[core, zz].reshape(4 * rows, units), other_down, preferred_element_type=jnp.float32
        )
        table = weights[core, zz].reshape(4 * rows, 128).astype(jnp.float32)
        weight = jnp.sum(jnp.where(mine, table, 0.0), axis=1, keepdims=True)
        return weight * value.astype(jnp.bfloat16).astype(jnp.float32)

    @pl.loop(0, depth)
    def _(t):
        zz = lax.rem(z + 1 + t, depth)
        a_out[t] = weighted(1 - n, zz).astype(jnp.bfloat16).reshape(2, 2 * rows, width)
        send_a(t).start()
        acc[...] = weighted(n, zz).reshape(2, 2 * rows, width)
        send_a(t).wait_recv()
        y_out[t] = (acc[1 - y] + a_in[t, 1 - y].astype(jnp.float32)).astype(jnp.bfloat16)
        send_y(t).start()
        keep[t] = acc[y] + a_in[t, y].astype(jnp.float32)

    @pl.loop(0, depth - 1)
    def _(t):
        send_y(t).wait_recv()
        z_out[t] = (keep[t] + y_in[t].astype(jnp.float32)).astype(jnp.bfloat16)
        send_z(t).start()

    last = depth - 1
    send_y(last).wait_recv()
    keep[last] += y_in[last].astype(jnp.float32)

    @pl.loop(0, last)
    def _(t):
        send_z(t).wait_recv()
        keep[last] += z_in[t].astype(jnp.float32)

    f_out[...] = keep[last].astype(jnp.bfloat16).reshape(2, rows, width)
    cross = remote(f_out.at[1 - x], f_in, f_send.at[0], f_recv.at[0], x_side)
    cross.start()
    cross.wait()
    mine_out = f_out[x]
    received = f_in[...]
    out[:, :width] = jnp.where(x == 0, mine_out, received)
    out[:, width:] = jnp.where(x == 0, received, mine_out)

    @pl.loop(0, depth)
    def _(t):
        send_a(t).wait_send()
        send_y(t).wait_send()

    @pl.loop(0, last)
    def _(t):
        send_z(t).wait_send()


def combine(own, other, weights, down, depth):
    rows, units = own.shape[4:]
    width = down.shape[1]
    experts = 4 * depth
    dma = pltpu.SemaphoreType.DMA
    vmem = pl.BlockSpec(memory_space=pltpu.VMEM)
    total = 8 * depth * rows
    half = (depth, 2 * rows, width)
    return pl.pallas_call(
        functools.partial(combine_kernel, depth, experts),
        out_shape=jax.ShapeDtypeStruct((rows, 2 * width), jnp.bfloat16),
        in_specs=[vmem] * 4,
        out_specs=vmem,
        scratch_shapes=[
            pltpu.VMEM((depth, 2, 2 * rows, width), jnp.bfloat16),
            pltpu.VMEM((depth, 2, 2 * rows, width), jnp.bfloat16),
            pltpu.VMEM((2, 2 * rows, width), jnp.float32),
            pltpu.VMEM(half, jnp.float32),
            pltpu.VMEM(half, jnp.bfloat16),
            pltpu.VMEM(half, jnp.bfloat16),
            pltpu.VMEM(half, jnp.bfloat16),
            pltpu.VMEM(half, jnp.bfloat16),
            pltpu.VMEM((2, rows, width), jnp.bfloat16),
            pltpu.VMEM((rows, width), jnp.bfloat16),
            dma((depth,)), dma((depth,)), dma((depth,)), dma((depth,)), dma((depth,)), dma((depth,)),
            dma((1,)), dma((1,)),
        ],
        cost_estimate=pl.CostEstimate(
            flops=4 * total * units * width, bytes_accessed=4 * total * units, transcendentals=0
        ),
        compiler_params=pltpu.CompilerParams(
            collective_id=1, has_side_effects=True, vmem_limit_bytes=60 * 1024 * 1024
        ),
    )(own, other, weights, down)


def per_device(tokens, routes, gate_weights, gate_proj, up_proj, down_proj):
    depth = lax.axis_size("z")
    pair_count = 2 * depth
    experts = 2 * pair_count
    rows = tokens.shape[0]
    expert_ids = jnp.arange(experts, dtype=jnp.int32)
    chosen = routes[:, :, None] == expert_ids[None, None, :]
    table = jnp.sum(jnp.where(chosen, gate_weights[:, :, None], 0.0), axis=1)
    high = lax.reduce_precision(table, 8, 7)
    middle = lax.reduce_precision(table - high, 8, 7)
    low = table - high - middle
    spare = jnp.zeros((rows, 128 - 3 * experts), jnp.float32)
    columns = jnp.concatenate([high, middle, low, spare], axis=1).astype(jnp.bfloat16)
    packed = jnp.concatenate([tokens, columns], axis=1)
    own_half, other_half, weights = gather_hidden(packed, gate_proj[0], up_proj[0], depth)
    return combine(own_half, other_half, weights, down_proj[0], depth)


def solution(mesh):
    sizes = dict(mesh.shape)
    devices = mesh.devices.reshape(sizes["parts"], sizes["node"], sizes["local"] // 4, 2, 2)
    split = Mesh(devices, ("parts", "node", "z", "y", "half"))
    rows = P(("parts", "node", "z", "y", "half"), None)
    blocks = P(("node", "z", "y", "half"), None, None)
    return jax.shard_map(
        per_device,
        mesh=split,
        in_specs=(rows, rows, rows, blocks, blocks, blocks),
        out_specs=rows,
        check_vma=False,
    )
```

```python
import functools

import jax
import jax.numpy as jnp
from jax import lax
from jax.experimental import pallas as pl
from jax.experimental.pallas import tpu as pltpu
from jax.sharding import Mesh, PartitionSpec as P

MESH = pl.DeviceIdType.MESH


def gather_kernel(
    depth, width, tok, gate, up, own_out, other_out, weight_out,
    buf, hid, gate_v, up_v,
    z_send, z_recv, x_send, x_recv, y_send, y_recv, s_send, s_recv,
    d_send, d_recv, load_sem, h_send, h_recv, o_sem, w_sem,
):
    p = lax.axis_index("parts")
    n = lax.axis_index("node")
    z = lax.axis_index("z")
    y = lax.axis_index("y")
    x = lax.axis_index("half")
    rows = tok.shape[0]
    sibling = (p, 1 - n, z, y, x)
    x_side = (p, n, z, y, 1 - x)
    y_side = (p, n, z, 1 - y, x)
    z_peers = [(p, n, lax.rem(z + step, depth), y, x) for step in range(1, depth)]

    barrier = pltpu.get_barrier_semaphore()
    for peer in [sibling, x_side, y_side] + z_peers:
        pl.semaphore_signal(barrier, inc=1, device_id=peer, device_id_type=MESH)
    pl.semaphore_wait(barrier, depth + 2)

    def remote(src, dst, send, recv, peer):
        return pltpu.make_async_remote_copy(
            src_ref=src, dst_ref=dst, send_sem=send, recv_sem=recv,
            device_id=peer, device_id_type=MESH,
        )

    def place(core, k, step):
        return buf.at[
            core, lax.rem(y + k // 2, 2), lax.rem(x + k % 2, 2), lax.rem(z - step + depth, depth)
        ]

    via_x = [step for step in range(depth) if step < depth // 4]

    def send_z(step):
        return remote(tok, place(n, 0, 0), z_send.at[step], z_recv.at[step], z_peers[step - 1])

    def recv_z(step):
        ref = place(n, 0, step)
        return remote(ref, ref, z_send.at[step], z_recv.at[step], sibling)

    def send_x(step):
        src = tok if step == 0 else place(n, 0, step)
        return remote(src, place(n, 0, step), x_send.at[step], x_recv.at[step], x_side)

    def send_y(step):
        src = tok if step == 0 else place(n, 0, step)
        return remote(src, place(n, 0, step), y_send.at[step], y_recv.at[step], y_side)

    def send_s(k, step):
        src = tok if (k == 0 and step == 0) else place(n, k, step)
        return remote(src, place(n, k, step), s_send.at[k, step], s_recv.at[k, step], sibling)

    def send_d(step):
        if step in via_x:
            ref, peer = place(n, 2, step), x_side
        else:
            ref, peer = place(n, 1, step), y_side
        return remote(ref, ref, d_send.at[step], d_recv.at[step], peer)

    def arrive(core, k, step, send, recv):
        ref = place(core, k, step)
        remote(ref, ref, send, recv, sibling).wait_recv()

    for step in range(1, depth):
        send_z(step).start()
    send_x(0).start()
    send_y(0).start()
    send_s(0, 0).start()
    own_copy = pltpu.make_async_copy(tok, place(n, 0, 0), load_sem.at[0])
    own_copy.start()
    gate_copy = pltpu.make_async_copy(gate, gate_v, load_sem.at[1])
    gate_copy.start()
    up_copy = pltpu.make_async_copy(up, up_v, load_sem.at[2])
    up_copy.start()

    def hid_copy(slot, core, yy, xx):
        return remote(
            hid.at[slot], other_out.at[core, :, yy, xx], h_send.at[slot], h_recv.at[slot], x_side
        )

    def out_copy(slot, core, yy, xx):
        return pltpu.make_async_copy(hid.at[slot], own_out.at[core, :, yy, xx], o_sem.at[slot])

    def weight_copy(slot, core, yy, xx):
        return pltpu.make_async_copy(
            buf.at[core, yy, xx, :, :, pl.ds(width, 128)],
            weight_out.at[core, :, yy, xx],
            w_sem.at[slot],
        )

    def group_of(slot):
        k = slot // 2
        core = lax.rem(n + slot % 2, 2)
        return core, lax.rem(y + k // 2, 2), lax.rem(x + k % 2, 2)

    def work(first, last):
        @pl.loop(first, last)
        def _(slot):
            core, yy, xx = group_of(slot)

            @pl.when(slot % 2 == 1)
            def _():
                for step in range(depth):
                    arrive(1 - n, slot // 2, step, s_send.at[slot // 2, step], s_recv.at[slot // 2, step])

            block = buf[core, yy, xx, :, :, pl.ds(0, width)].reshape(depth * rows, width)
            gate_act = jnp.dot(block, gate_v[...], preferred_element_type=jnp.float32)
            up_act = jnp.dot(block, up_v[...], preferred_element_type=jnp.float32)
            hidden = gate_act / (1.0 + jnp.exp(-gate_act)) * up_act
            hid[slot] = hidden.astype(jnp.bfloat16).reshape(depth, rows, hidden.shape[1])
            hid_copy(slot, core, yy, xx).start()
            out_copy(slot, core, yy, xx).start()
            weight_copy(slot, core, yy, xx).start()

    for step in range(1, depth + 2):
        if step < depth:
            recv_z(step).wait_recv()
            send_x(step).start()
            send_y(step).start()
            send_s(0, step).start()
        if 1 <= step <= depth:
            late = step - 1
            arrive(n, 1, late, x_send.at[late], x_recv.at[late])
            if late not in via_x:
                send_d(late).start()
            send_s(1, late).start()
            arrive(n, 2, late, y_send.at[late], y_recv.at[late])
            if late in via_x:
                send_d(late).start()
            send_s(2, late).start()
        if step == depth - 1:
            own_copy.wait()
            gate_copy.wait()
            up_copy.wait()
            work(0, 2)
        if step == depth:
            work(2, 6)
        if step >= 2:
            late = step - 2
            arrive(n, 3, late, d_send.at[late], d_recv.at[late])
            send_s(3, late).start()
    work(6, 8)

    for step in range(1, depth):
        send_z(step).wait_send()
    for step in range(depth):
        send_x(step).wait_send()
        send_y(step).wait_send()
        send_d(step).wait_send()
        for k in range(4):
            send_s(k, step).wait_send()

    @pl.loop(0, 8)
    def _(slot):
        core, yy, xx = group_of(slot)
        hid_copy(slot, core, yy, xx).wait_send()
        hid_copy(slot, core, yy, lax.rem(xx + 1, 2)).wait_recv()
        out_copy(slot, core, yy, xx).wait()
        weight_copy(slot, core, yy, xx).wait()


def gather_hidden(packed, gate, up, depth):
    rows, wide = packed.shape
    width, units = gate.shape
    grid = (2, depth, 2, 2, rows)
    dma = pltpu.SemaphoreType.DMA
    any_spec = pl.BlockSpec(memory_space=pl.ANY)
    total = 8 * depth * rows
    return pl.pallas_call(
        functools.partial(gather_kernel, depth, width),
        out_shape=(
            jax.ShapeDtypeStruct(grid + (units,), jnp.bfloat16),
            jax.ShapeDtypeStruct(grid + (units,), jnp.bfloat16),
            jax.ShapeDtypeStruct(grid + (128,), jnp.bfloat16),
        ),
        in_specs=[any_spec] * 3,
        out_specs=(any_spec,) * 3,
        scratch_shapes=[
            pltpu.VMEM((2, 2, 2, depth, rows, wide), jnp.bfloat16),
            pltpu.VMEM((8, depth, rows, units), jnp.bfloat16),
            pltpu.VMEM((width, units), jnp.bfloat16),
            pltpu.VMEM((width, units), jnp.bfloat16),
            dma((depth,)), dma((depth,)), dma((depth,)), dma((depth,)), dma((depth,)), dma((depth,)),
            dma((4, depth)), dma((4, depth)), dma((depth,)), dma((depth,)),
            dma((3,)), dma((8,)), dma((8,)), dma((8,)), dma((8,)),
        ],
        cost_estimate=pl.CostEstimate(
            flops=4 * total * width * units, bytes_accessed=2 * total * wide, transcendentals=total * units
        ),
        compiler_params=pltpu.CompilerParams(
            collective_id=0, has_side_effects=True, vmem_limit_bytes=56 * 1024 * 1024
        ),
    )(packed, gate, up)


def combine_kernel(
    depth, experts, own, other, weights, down, out,
    a_out, a_in, acc, keep, y_out, y_in, z_out, z_in, f_out, f_in,
    a_send, a_recv, y_send, y_recv, z_send, z_recv, f_send, f_recv,
):
    p = lax.axis_index("parts")
    n = lax.axis_index("node")
    z = lax.axis_index("z")
    y = lax.axis_index("y")
    x = lax.axis_index("half")
    rows, units = own.shape[4:]
    width = down.shape[1]
    sibling = (p, 1 - n, z, y, x)
    x_side = (p, n, z, y, 1 - x)
    y_side = (p, n, z, 1 - y, x)

    barrier = pltpu.get_barrier_semaphore()
    for peer in [sibling, x_side, y_side] + [
        (p, n, lax.rem(z + step, depth), y, x) for step in range(1, depth)
    ]:
        pl.semaphore_signal(barrier, inc=1, device_id=peer, device_id_type=MESH)
    pl.semaphore_wait(barrier, depth + 2)

    def remote(src, dst, send, recv, peer):
        return pltpu.make_async_remote_copy(
            src_ref=src, dst_ref=dst, send_sem=send, recv_sem=recv,
            device_id=peer, device_id_type=MESH,
        )

    def send_a(t):
        return remote(a_out.at[t], a_in.at[t], a_send.at[t], a_recv.at[t], sibling)

    def send_y(t):
        return remote(y_out.at[t], y_in.at[t], y_send.at[t], y_recv.at[t], y_side)

    def send_z(t):
        peer = (p, n, lax.rem(z + 1 + t, depth), y, x)
        return remote(z_out.at[t], z_in.at[t], z_send.at[t], z_recv.at[t], peer)

    expert = (n * depth + z) * 2 + y
    lane = lax.broadcasted_iota(jnp.int32, (4 * rows, 128), 1)
    mine = (lane == expert) | (lane == expert + experts) | (lane == expert + 2 * experts)

    def weighted(core, zz):
        own_down = down[pl.ds(pl.multiple_of(x * units, units), units), :]
        other_down = down[pl.ds(pl.multiple_of((1 - x) * units, units), units), :]
        value = jnp.dot(
            own[core, zz].reshape(4 * rows, units), own_down, preferred_element_type=jnp.float32
        ) + jnp.dot(
            other[core, zz].reshape(4 * rows, units), other_down, preferred_element_type=jnp.float32
        )
        table = weights[core, zz].reshape(4 * rows, 128).astype(jnp.float32)
        weight = jnp.sum(jnp.where(mine, table, 0.0), axis=1, keepdims=True)
        return weight * value.astype(jnp.bfloat16).astype(jnp.float32)

    @pl.loop(0, depth)
    def _(t):
        zz = lax.rem(z + 1 + t, depth)
        a_out[t] = weighted(1 - n, zz).astype(jnp.bfloat16).reshape(2, 2 * rows, width)
        send_a(t).start()
        acc[...] = weighted(n, zz).reshape(2, 2 * rows, width)
        send_a(t).wait_recv()
        y_out[t] = (acc[1 - y] + a_in[t, 1 - y].astype(jnp.float32)).astype(jnp.bfloat16)
        send_y(t).start()
        keep[t] = acc[y] + a_in[t, y].astype(jnp.float32)

    @pl.loop(0, depth - 1)
    def _(t):
        send_y(t).wait_recv()
        z_out[t] = (keep[t] + y_in[t].astype(jnp.float32)).astype(jnp.bfloat16)
        send_z(t).start()

    last = depth - 1
    send_y(last).wait_recv()
    keep[last] += y_in[last].astype(jnp.float32)

    @pl.loop(0, last)
    def _(t):
        send_z(t).wait_recv()
        keep[last] += z_in[t].astype(jnp.float32)

    f_out[...] = keep[last].astype(jnp.bfloat16).reshape(2, rows, width)
    cross = remote(f_out.at[1 - x], f_in, f_send.at[0], f_recv.at[0], x_side)
    cross.start()
    cross.wait()
    mine_out = f_out[x]
    received = f_in[...]
    out[:, :width] = jnp.where(x == 0, mine_out, received)
    out[:, width:] = jnp.where(x == 0, received, mine_out)

    @pl.loop(0, depth)
    def _(t):
        send_a(t).wait_send()
        send_y(t).wait_send()

    @pl.loop(0, last)
    def _(t):
        send_z(t).wait_send()


def combine(own, other, weights, down, depth):
    rows, units = own.shape[4:]
    width = down.shape[1]
    experts = 4 * depth
    dma = pltpu.SemaphoreType.DMA
    vmem = pl.BlockSpec(memory_space=pltpu.VMEM)
    total = 8 * depth * rows
    half = (depth, 2 * rows, width)
    return pl.pallas_call(
        functools.partial(combine_kernel, depth, experts),
        out_shape=jax.ShapeDtypeStruct((rows, 2 * width), jnp.bfloat16),
        in_specs=[vmem] * 4,
        out_specs=vmem,
        scratch_shapes=[
            pltpu.VMEM((depth, 2, 2 * rows, width), jnp.bfloat16),
            pltpu.VMEM((depth, 2, 2 * rows, width), jnp.bfloat16),
            pltpu.VMEM((2, 2 * rows, width), jnp.float32),
            pltpu.VMEM(half, jnp.float32),
            pltpu.VMEM(half, jnp.bfloat16),
            pltpu.VMEM(half, jnp.bfloat16),
            pltpu.VMEM(half, jnp.bfloat16),
            pltpu.VMEM(half, jnp.bfloat16),
            pltpu.VMEM((2, rows, width), jnp.bfloat16),
            pltpu.VMEM((rows, width), jnp.bfloat16),
            dma((depth,)), dma((depth,)), dma((depth,)), dma((depth,)), dma((depth,)), dma((depth,)),
            dma((1,)), dma((1,)),
        ],
        cost_estimate=pl.CostEstimate(
            flops=4 * total * units * width, bytes_accessed=4 * total * units, transcendentals=0
        ),
        compiler_params=pltpu.CompilerParams(
            collective_id=1, has_side_effects=True, vmem_limit_bytes=60 * 1024 * 1024
        ),
    )(own, other, weights, down)


def per_device(tokens, routes, gate_weights, gate_proj, up_proj, down_proj):
    depth = lax.axis_size("z")
    pair_count = 2 * depth
    experts = 2 * pair_count
    rows = tokens.shape[0]
    expert_ids = jnp.arange(experts, dtype=jnp.int32)
    chosen = routes[:, :, None] == expert_ids[None, None, :]
    table = jnp.sum(jnp.where(chosen, gate_weights[:, :, None], 0.0), axis=1)
    high = lax.reduce_precision(table, 8, 7)
    middle = lax.reduce_precision(table - high, 8, 7)
    low = table - high - middle
    spare = jnp.zeros((rows, 128 - 3 * experts), jnp.float32)
    columns = jnp.concatenate([high, middle, low, spare], axis=1).astype(jnp.bfloat16)
    packed = jnp.concatenate([tokens, columns], axis=1)
    own_half, other_half, weights = gather_hidden(packed, gate_proj[0], up_proj[0], depth)
    return combine(own_half, other_half, weights, down_proj[0], depth)


def solution(mesh):
    sizes = dict(mesh.shape)
    devices = mesh.devices.reshape(sizes["parts"], sizes["node"], sizes["local"] // 4, 2, 2)
    split = Mesh(devices, ("parts", "node", "z", "y", "half"))
    rows = P(("parts", "node", "z", "y", "half"), None)
    blocks = P(("node", "z", "y", "half"), None, None)
    return jax.shard_map(
        per_device,
        mesh=split,
        in_specs=(rows, rows, rows, blocks, blocks, blocks),
        out_specs=rows,
        check_vma=False,
    )
```

```python
import functools

import jax
import jax.numpy as jnp
from jax import lax
from jax.experimental import pallas as pl
from jax.experimental.pallas import tpu as pltpu
from jax.sharding import Mesh, PartitionSpec as P

MESH = pl.DeviceIdType.MESH


def gather_kernel(
    depth, width, tok, gate, up, own_out, other_out, weight_out,
    buf, hid, gate_v, up_v,
    z_send, z_recv, x_send, x_recv, y_send, y_recv, s_send, s_recv,
    d_send, d_recv, load_sem, h_send, h_recv, o_sem, w_sem,
):
    p = lax.axis_index("parts")
    n = lax.axis_index("node")
    z = lax.axis_index("z")
    y = lax.axis_index("y")
    x = lax.axis_index("half")
    rows = tok.shape[0]
    sibling = (p, 1 - n, z, y, x)
    x_side = (p, n, z, y, 1 - x)
    y_side = (p, n, z, 1 - y, x)
    z_peers = [(p, n, lax.rem(z + step, depth), y, x) for step in range(1, depth)]

    barrier = pltpu.get_barrier_semaphore()
    for peer in [sibling, x_side, y_side] + z_peers:
        pl.semaphore_signal(barrier, inc=1, device_id=peer, device_id_type=MESH)
    pl.semaphore_wait(barrier, depth + 2)

    def remote(src, dst, send, recv, peer):
        return pltpu.make_async_remote_copy(
            src_ref=src, dst_ref=dst, send_sem=send, recv_sem=recv,
            device_id=peer, device_id_type=MESH,
        )

    def place(core, k, step):
        return buf.at[
            core, lax.rem(y + k // 2, 2), lax.rem(x + k % 2, 2), lax.rem(z - step + depth, depth)
        ]

    via_x = [step for step in range(depth) if step < depth // 4]

    def send_z(step):
        return remote(tok, place(n, 0, 0), z_send.at[step], z_recv.at[step], z_peers[step - 1])

    def recv_z(step):
        ref = place(n, 0, step)
        return remote(ref, ref, z_send.at[step], z_recv.at[step], sibling)

    def send_x(step):
        src = tok if step == 0 else place(n, 0, step)
        return remote(src, place(n, 0, step), x_send.at[step], x_recv.at[step], x_side)

    def send_y(step):
        src = tok if step == 0 else place(n, 0, step)
        return remote(src, place(n, 0, step), y_send.at[step], y_recv.at[step], y_side)

    def send_s(k, step):
        src = tok if (k == 0 and step == 0) else place(n, k, step)
        return remote(src, place(n, k, step), s_send.at[k, step], s_recv.at[k, step], sibling)

    def send_d(step):
        if step in via_x:
            ref, peer = place(n, 2, step), x_side
        else:
            ref, peer = place(n, 1, step), y_side
        return remote(ref, ref, d_send.at[step], d_recv.at[step], peer)

    def arrive(core, k, step, send, recv):
        ref = place(core, k, step)
        remote(ref, ref, send, recv, sibling).wait_recv()

    for step in range(1, depth):
        send_z(step).start()
    send_x(0).start()
    send_y(0).start()
    send_s(0, 0).start()
    own_copy = pltpu.make_async_copy(tok, place(n, 0, 0), load_sem.at[0])
    own_copy.start()
    gate_copy = pltpu.make_async_copy(gate, gate_v, load_sem.at[1])
    gate_copy.start()
    up_copy = pltpu.make_async_copy(up, up_v, load_sem.at[2])
    up_copy.start()

    def hid_copy(slot, core, yy, xx):
        return remote(
            hid.at[slot], other_out.at[core, :, yy, xx], h_send.at[slot], h_recv.at[slot], x_side
        )

    def out_copy(slot, core, yy, xx):
        return pltpu.make_async_copy(hid.at[slot], own_out.at[core, :, yy, xx], o_sem.at[slot])

    def weight_copy(slot, core, yy, xx):
        return pltpu.make_async_copy(
            buf.at[core, yy, xx, :, :, pl.ds(width, 128)],
            weight_out.at[core, :, yy, xx],
            w_sem.at[slot],
        )

    def group_of(slot):
        k = slot // 2
        core = lax.rem(n + slot % 2, 2)
        return core, lax.rem(y + k // 2, 2), lax.rem(x + k % 2, 2)

    def work(first, last):
        @pl.loop(first, last)
        def _(slot):
            core, yy, xx = group_of(slot)

            @pl.when(slot % 2 == 1)
            def _():
                for step in range(depth):
                    arrive(1 - n, slot // 2, step, s_send.at[slot // 2, step], s_recv.at[slot // 2, step])

            block = buf[core, yy, xx, :, :, pl.ds(0, width)].reshape(depth * rows, width)
            gate_act = jnp.dot(block, gate_v[...], preferred_element_type=jnp.float32)
            up_act = jnp.dot(block, up_v[...], preferred_element_type=jnp.float32)
            hidden = gate_act / (1.0 + jnp.exp(-gate_act)) * up_act
            hid[slot] = hidden.astype(jnp.bfloat16).reshape(depth, rows, hidden.shape[1])
            hid_copy(slot, core, yy, xx).start()
            out_copy(slot, core, yy, xx).start()
            weight_copy(slot, core, yy, xx).start()

    for step in range(1, depth + 2):
        if step < depth:
            recv_z(step).wait_recv()
            send_x(step).start()
            send_y(step).start()
            send_s(0, step).start()
        if 1 <= step <= depth:
            late = step - 1
            arrive(n, 1, late, x_send.at[late], x_recv.at[late])
            if late not in via_x:
                send_d(late).start()
            send_s(1, late).start()
            arrive(n, 2, late, y_send.at[late], y_recv.at[late])
            if late in via_x:
                send_d(late).start()
            send_s(2, late).start()
        if step == depth - 1:
            own_copy.wait()
            gate_copy.wait()
            up_copy.wait()
            work(0, 2)
        if step == depth:
            work(2, 6)
        if step >= 2:
            late = step - 2
            arrive(n, 3, late, d_send.at[late], d_recv.at[late])
            send_s(3, late).start()
    work(6, 8)

    for step in range(1, depth):
        send_z(step).wait_send()
    for step in range(depth):
        send_x(step).wait_send()
        send_y(step).wait_send()
        send_d(step).wait_send()
        for k in range(4):
            send_s(k, step).wait_send()

    @pl.loop(0, 8)
    def _(slot):
        core, yy, xx = group_of(slot)
        hid_copy(slot, core, yy, xx).wait_send()
        hid_copy(slot, core, yy, lax.rem(xx + 1, 2)).wait_recv()
        out_copy(slot, core, yy, xx).wait()
        weight_copy(slot, core, yy, xx).wait()


def gather_hidden(packed, gate, up, depth):
    rows, wide = packed.shape
    width, units = gate.shape
    grid = (2, depth, 2, 2, rows)
    dma = pltpu.SemaphoreType.DMA
    any_spec = pl.BlockSpec(memory_space=pl.ANY)
    total = 8 * depth * rows
    return pl.pallas_call(
        functools.partial(gather_kernel, depth, width),
        out_shape=(
            jax.ShapeDtypeStruct(grid + (units,), jnp.bfloat16),
            jax.ShapeDtypeStruct(grid + (units,), jnp.bfloat16),
            jax.ShapeDtypeStruct(grid + (128,), jnp.bfloat16),
        ),
        in_specs=[any_spec] * 3,
        out_specs=(any_spec,) * 3,
        scratch_shapes=[
            pltpu.VMEM((2, 2, 2, depth, rows, wide), jnp.bfloat16),
            pltpu.VMEM((8, depth, rows, units), jnp.bfloat16),
            pltpu.VMEM((width, units), jnp.bfloat16),
            pltpu.VMEM((width, units), jnp.bfloat16),
            dma((depth,)), dma((depth,)), dma((depth,)), dma((depth,)), dma((depth,)), dma((depth,)),
            dma((4, depth)), dma((4, depth)), dma((depth,)), dma((depth,)),
            dma((3,)), dma((8,)), dma((8,)), dma((8,)), dma((8,)),
        ],
        cost_estimate=pl.CostEstimate(
            flops=4 * total * width * units, bytes_accessed=2 * total * wide, transcendentals=total * units
        ),
        compiler_params=pltpu.CompilerParams(
            collective_id=0, has_side_effects=True, vmem_limit_bytes=56 * 1024 * 1024
        ),
    )(packed, gate, up)


def combine_kernel(
    depth, experts, own, other, weights, down, out,
    a_out, a_in, acc, keep, y_out, y_in, z_out, z_in, f_out, f_in,
    a_send, a_recv, y_send, y_recv, z_send, z_recv, f_send, f_recv,
):
    p = lax.axis_index("parts")
    n = lax.axis_index("node")
    z = lax.axis_index("z")
    y = lax.axis_index("y")
    x = lax.axis_index("half")
    rows, units = own.shape[4:]
    width = down.shape[1]
    sibling = (p, 1 - n, z, y, x)
    x_side = (p, n, z, y, 1 - x)
    y_side = (p, n, z, 1 - y, x)

    barrier = pltpu.get_barrier_semaphore()
    for peer in [sibling, x_side, y_side] + [
        (p, n, lax.rem(z + step, depth), y, x) for step in range(1, depth)
    ]:
        pl.semaphore_signal(barrier, inc=1, device_id=peer, device_id_type=MESH)
    pl.semaphore_wait(barrier, depth + 2)

    def remote(src, dst, send, recv, peer):
        return pltpu.make_async_remote_copy(
            src_ref=src, dst_ref=dst, send_sem=send, recv_sem=recv,
            device_id=peer, device_id_type=MESH,
        )

    def send_a(t):
        return remote(a_out.at[t], a_in.at[t], a_send.at[t], a_recv.at[t], sibling)

    def send_y(t):
        return remote(y_out.at[t], y_in.at[t], y_send.at[t], y_recv.at[t], y_side)

    def send_z(t):
        peer = (p, n, lax.rem(z + 1 + t, depth), y, x)
        return remote(z_out.at[t], z_in.at[t], z_send.at[t], z_recv.at[t], peer)

    expert = (n * depth + z) * 2 + y
    lane = lax.broadcasted_iota(jnp.int32, (4 * rows, 128), 1)
    mine = (lane == expert) | (lane == expert + experts) | (lane == expert + 2 * experts)

    def weighted(core, zz):
        own_down = down[pl.ds(pl.multiple_of(x * units, units), units), :]
        other_down = down[pl.ds(pl.multiple_of((1 - x) * units, units), units), :]
        value = jnp.dot(
            own[core, zz].reshape(4 * rows, units), own_down, preferred_element_type=jnp.float32
        ) + jnp.dot(
            other[core, zz].reshape(4 * rows, units), other_down, preferred_element_type=jnp.float32
        )
        table = weights[core, zz].reshape(4 * rows, 128).astype(jnp.float32)
        weight = jnp.sum(jnp.where(mine, table, 0.0), axis=1, keepdims=True)
        return weight * value.astype(jnp.bfloat16).astype(jnp.float32)

    def pass_on(t):
        send_y(t).wait_recv()
        z_out[t] = (keep[t] + y_in[t].astype(jnp.float32)).astype(jnp.bfloat16)
        send_z(t).start()

    @pl.loop(0, depth)
    def _(t):
        zz = lax.rem(z + 1 + t, depth)
        a_out[t] = weighted(1 - n, zz).astype(jnp.bfloat16).reshape(2, 2 * rows, width)
        send_a(t).start()
        acc[...] = weighted(n, zz).reshape(2, 2 * rows, width)
        send_a(t).wait_recv()
        y_out[t] = (acc[1 - y] + a_in[t, 1 - y].astype(jnp.float32)).astype(jnp.bfloat16)
        send_y(t).start()
        keep[t] = acc[y] + a_in[t, y].astype(jnp.float32)

        @pl.when(t >= 2)
        def _():
            pass_on(t - 2)

    @pl.loop(depth - 2, depth - 1)
    def _(t):
        pass_on(t)

    last = depth - 1
    send_y(last).wait_recv()
    keep[last] += y_in[last].astype(jnp.float32)

    @pl.loop(0, last)
    def _(t):
        send_z(t).wait_recv()
        keep[last] += z_in[t].astype(jnp.float32)

    f_out[...] = keep[last].astype(jnp.bfloat16).reshape(2, rows, width)
    cross = remote(f_out.at[1 - x], f_in, f_send.at[0], f_recv.at[0], x_side)
    cross.start()
    cross.wait()
    mine_out = f_out[x]
    received = f_in[...]
    out[:, :width] = jnp.where(x == 0, mine_out, received)
    out[:, width:] = jnp.where(x == 0, received, mine_out)

    @pl.loop(0, depth)
    def _(t):
        send_a(t).wait_send()
        send_y(t).wait_send()

    @pl.loop(0, last)
    def _(t):
        send_z(t).wait_send()


def combine(own, other, weights, down, depth):
    rows, units = own.shape[4:]
    width = down.shape[1]
    experts = 4 * depth
    dma = pltpu.SemaphoreType.DMA
    vmem = pl.BlockSpec(memory_space=pltpu.VMEM)
    total = 8 * depth * rows
    half = (depth, 2 * rows, width)
    return pl.pallas_call(
        functools.partial(combine_kernel, depth, experts),
        out_shape=jax.ShapeDtypeStruct((rows, 2 * width), jnp.bfloat16),
        in_specs=[vmem] * 4,
        out_specs=vmem,
        scratch_shapes=[
            pltpu.VMEM((depth, 2, 2 * rows, width), jnp.bfloat16),
            pltpu.VMEM((depth, 2, 2 * rows, width), jnp.bfloat16),
            pltpu.VMEM((2, 2 * rows, width), jnp.float32),
            pltpu.VMEM(half, jnp.float32),
            pltpu.VMEM(half, jnp.bfloat16),
            pltpu.VMEM(half, jnp.bfloat16),
            pltpu.VMEM(half, jnp.bfloat16),
            pltpu.VMEM(half, jnp.bfloat16),
            pltpu.VMEM((2, rows, width), jnp.bfloat16),
            pltpu.VMEM((rows, width), jnp.bfloat16),
            dma((depth,)), dma((depth,)), dma((depth,)), dma((depth,)), dma((depth,)), dma((depth,)),
            dma((1,)), dma((1,)),
        ],
        cost_estimate=pl.CostEstimate(
            flops=4 * total * units * width, bytes_accessed=4 * total * units, transcendentals=0
        ),
        compiler_params=pltpu.CompilerParams(
            collective_id=1, has_side_effects=True, vmem_limit_bytes=60 * 1024 * 1024
        ),
    )(own, other, weights, down)


def per_device(tokens, routes, gate_weights, gate_proj, up_proj, down_proj):
    depth = lax.axis_size("z")
    pair_count = 2 * depth
    experts = 2 * pair_count
    rows = tokens.shape[0]
    expert_ids = jnp.arange(experts, dtype=jnp.int32)
    chosen = routes[:, :, None] == expert_ids[None, None, :]
    table = jnp.sum(jnp.where(chosen, gate_weights[:, :, None], 0.0), axis=1)
    high = lax.reduce_precision(table, 8, 7)
    middle = lax.reduce_precision(table - high, 8, 7)
    low = table - high - middle
    spare = jnp.zeros((rows, 128 - 3 * experts), jnp.float32)
    columns = jnp.concatenate([high, middle, low, spare], axis=1).astype(jnp.bfloat16)
    packed = jnp.concatenate([tokens, columns], axis=1)
    own_half, other_half, weights = gather_hidden(packed, gate_proj[0], up_proj[0], depth)
    return combine(own_half, other_half, weights, down_proj[0], depth)


def solution(mesh):
    sizes = dict(mesh.shape)
    devices = mesh.devices.reshape(sizes["parts"], sizes["node"], sizes["local"] // 4, 2, 2)
    split = Mesh(devices, ("parts", "node", "z", "y", "half"))
    rows = P(("parts", "node", "z", "y", "half"), None)
    blocks = P(("node", "z", "y", "half"), None, None)
    return jax.shard_map(
        per_device,
        mesh=split,
        in_specs=(rows, rows, rows, blocks, blocks, blocks),
        out_specs=rows,
        check_vma=False,
    )
```
